256 devices in a mesh: gx: 8 (over x, y_lo), gy: 32 (over y_hi, z, core).
Axes of the slice: x: 4, y: 4 (y_hi: 2, y_lo: 2; y = y_hi * 2 + y_lo), z: 8, core: 2. Of those that a mesh axis runs over, the one named last changes fastest.
Arguments:
- state_field: bfloat16 [20, 64, 256, 256], P(None, 'gx', 'gy'), may hold values from -6 to 6
- conv_weight: bfloat16 [3, 20, 180], replicated, may hold values from -0.25 to 0.25
- spectral_weight: float32 [32, 32, 2, 20, 20, 16], P('gx', 'gy'), may hold values from -1 to 1
- channel_bias: float32 [20], replicated, may hold values from -3 to 3
Outputs:
- layer_out: bfloat16 [20, 64, 256, 256], P(None, 'gx', 'gy')
The draws below stay inside these ranges and needn't reach their ends.
All inputs are finite; a program needn't handle non-finite values.
Results may differ from the reference program's by a relative error of at most 0.0032.
Values may be sent and summed in bfloat16 or wider, within the bound.
A program may use at most 128 MiB of HBM per device.

```python
import math
import jax
import jax.numpy as jnp
from jax import lax

C = 20
NZ = 256
MX = 32
MY = 32
MZ = 16
NX = 64
NY = 256


def shard_levels(rng, extent, pieces, least, largest):
    def one(dim, parts):
        heights = jax.random.uniform(jax.random.fold_in(jax.random.fold_in(rng, 6), dim), (parts,), jnp.float32, least / len(pieces), largest / len(pieces))
        return jnp.repeat(jnp.exp(heights), extent[dim] // parts).reshape((-1,) + (1,) * (len(extent) - dim - 1))

    loudness = one(*pieces[0])
    for cut in pieces[1:]:
        loudness = loudness * one(*cut)
    return loudness


def centred(key, shape, width, limit, shards=(), held_as=jnp.bfloat16):
    level = shard_levels(key, shape, shards, -0.22, 0.18) if shards else 1.0
    values = jax.random.normal(key, shape, jnp.float32) * width * level
    return jnp.minimum(jnp.maximum(values, -limit), limit).astype(held_as)


def setup_inputs(seed: int = 0) -> dict:
    key_of = jax.random.split(jax.random.key(seed), 5)
    return {
        "state_field": centred(key_of[0], (C, NX, NY, NZ), 1.0, 6.0, ((1, 8), (2, 32))),
        "conv_weight": centred(key_of[1], (3, C, 9 * C), (27 * C) ** -0.5, 0.25),
        "spectral_weight": centred(key_of[2], (MX, MY, 2, C, C, MZ), (2 * C) ** -0.5, 1.0, ((0, 8), (1, 32)), jnp.float32),
        "channel_bias": centred(key_of[3], (C,), 0.5, 3.0, (), jnp.float32),
    }


def twiddle(freq_rows, positions, length, mode_count):
    freq = jnp.where(freq_rows < mode_count // 2, freq_rows, freq_rows - mode_count)
    angle_int = freq[:, None] * positions[None, :] % length
    angle = 2.0 * jnp.pi * angle_int.astype(jnp.float32) / length
    return (jnp.cos(angle), jnp.sin(angle))

def forward_mix(form, cos_tab, sin_tab, real_part, imag_part):
    highest = lax.Precision.HIGHEST
    new_real = jnp.einsum(form, cos_tab, real_part, precision=highest) + jnp.einsum(form, sin_tab, imag_part, precision=highest)
    new_imag = jnp.einsum(form, cos_tab, imag_part, precision=highest) - jnp.einsum(form, sin_tab, real_part, precision=highest)
    return (new_real, new_imag)

def inverse_mix(form, cos_tab, sin_tab, real_part, imag_part):
    highest = lax.Precision.HIGHEST
    new_real = jnp.einsum(form, cos_tab, real_part, precision=highest) - jnp.einsum(form, sin_tab, imag_part, precision=highest)
    new_imag = jnp.einsum(form, cos_tab, imag_part, precision=highest) + jnp.einsum(form, sin_tab, real_part, precision=highest)
    return (new_real, new_imag)

def reference(state_field, conv_weight, spectral_weight, channel_bias):
    highest = lax.Precision.HIGHEST
    conv_sum = jnp.zeros((C, NX, NY, NZ), jnp.float32)
    for shift_x in range(3):
        for shift_y in range(3):
            for shift_z in range(3):
                moved = jnp.roll(state_field, (1 - shift_x, 1 - shift_y, 1 - shift_z), axis=(1, 2, 3))
                offset = (shift_y * 3 + shift_z) * C
                kernel = conv_weight[shift_x][:, offset:offset + C]
                conv_sum = conv_sum + lax.dot_general(kernel, moved, (((1,), (0,)), ((), ())), preferred_element_type=jnp.float32)
    z_index = jnp.arange(NZ, dtype=jnp.int32)
    z_modes = jnp.arange(MZ, dtype=jnp.int32)
    z_angle = 2.0 * jnp.pi * (z_index[:, None] * z_modes[None, :] % NZ).astype(jnp.float32) / NZ
    z_table = jnp.concatenate([jnp.cos(z_angle), -jnp.sin(z_angle)], axis=1).astype(jnp.bfloat16)
    z_spectrum = jnp.dot(state_field.reshape(-1, NZ), z_table, preferred_element_type=jnp.float32).reshape(C, NX, NY, 2 * MZ)
    cos_y, sin_y = twiddle(jnp.arange(MY, dtype=jnp.int32), jnp.arange(NY, dtype=jnp.int32), NY, MY)
    cos_x, sin_x = twiddle(jnp.arange(MX, dtype=jnp.int32), jnp.arange(NX, dtype=jnp.int32), NX, MX)
    y_real, y_imag = forward_mix('jy,cxyz->jcxz', cos_y, sin_y, z_spectrum[..., :MZ], z_spectrum[..., MZ:])
    mode_real, mode_imag = forward_mix('kx,jcxz->kjcz', cos_x, sin_x, y_real, y_imag)
    weight_real = spectral_weight[:, :, 0]
    weight_imag = spectral_weight[:, :, 1]
    form = 'abioz,abiz->aboz'
    mixed_real = jnp.einsum(form, weight_real, mode_real, precision=highest) - jnp.einsum(form, weight_imag, mode_imag, precision=highest)
    mixed_imag = jnp.einsum(form, weight_real, mode_imag, precision=highest) + jnp.einsum(form, weight_imag, mode_real, precision=highest)
    back_real, back_imag = inverse_mix('kx,kjcz->jcxz', cos_x, sin_x, mixed_real, mixed_imag)
    grid_real, grid_imag = inverse_mix('jy,jcxz->cxyz', cos_y, sin_y, back_real, back_imag)
    grid_modes = jnp.concatenate([grid_real, grid_imag], axis=-1)
    scale_factor = 1.0 / math.sqrt(float(NX) * NY * NZ * 2.0 * MX * MY * MZ)
    weight_modes = jnp.where(z_modes == 0, 1.0, 2.0).astype(jnp.float32) * scale_factor
    back_angle = jnp.transpose(z_angle)
    back_table = jnp.concatenate([jnp.cos(back_angle) * weight_modes[:, None], -jnp.sin(back_angle) * weight_modes[:, None]], axis=0)
    spectral = jnp.dot(grid_modes.reshape(-1, 2 * MZ), back_table, precision=highest, preferred_element_type=jnp.float32).reshape(C, NX, NY, NZ)
    return jax.nn.gelu(conv_sum + spectral + channel_bias[:, None, None, None]).astype(jnp.bfloat16)
```

```python
import functools
import math

import jax
import jax.numpy as jnp
import ml_dtypes
import numpy as np
from jax import lax
from jax.experimental import pallas as pl
from jax.experimental.pallas import tpu as pltpu
from jax.sharding import PartitionSpec as P

MESH = pl.DeviceIdType.MESH
F32 = jnp.float32
BF16 = jnp.bfloat16
C = 20
NZ = 256
NX = 64
NY = 256
MX = 32
MY = 32
MZ = 16
GX = 8
GY = 32
LX = 8
LY = 8
ROWS = C * LY
GROUPS = 2 * C
PEERS = GX + GY - 2 + 4


def split(table):
    high = table.astype(np.float32).astype(ml_dtypes.bfloat16)
    low = (table - high.astype(np.float64)).astype(np.float32).astype(ml_dtypes.bfloat16)
    return np.stack([high, low])


def z_forward_table():
    z, k = np.arange(NZ)[:, None], np.arange(MZ)[None, :]
    angle = 2.0 * np.pi * (z * k % NZ) / NZ
    cos, sin = np.cos(angle), np.sin(angle)
    table = np.zeros((4, NZ, 2, 4, 2, MZ))
    for low in range(4):
        table[low, :, 0, low, 0] = cos
        table[low, :, 0, low, 1] = -sin
        table[low, :, 1, low, 0] = -sin
        table[low, :, 1, low, 1] = -cos
    return table.reshape(4 * NZ, 256).astype(np.float32).astype(ml_dtypes.bfloat16)


def z_inverse_table():
    k, z = np.arange(MZ)[:, None], np.arange(NZ)[None, :]
    angle = 2.0 * np.pi * (z * k % NZ) / NZ
    weight = np.where(k == 0, 1.0, 2.0) / math.sqrt(float(NX) * NY * NZ * 2.0 * MX * MY * MZ)
    cos, sin = np.cos(angle) * weight, np.sin(angle) * weight
    table = np.zeros((2, 4, 2, MZ, 4, NZ))
    for low in range(4):
        table[0, low, 0, :, low] = cos
        table[0, low, 1, :, low] = -sin
        table[1, low, 0, :, low] = -sin
        table[1, low, 1, :, low] = -cos
    return split(table.reshape(256, 4 * NZ))


def x_tables():
    kx = np.arange(MX)
    freq = np.where(kx < MX // 2, kx, kx - MX)
    angle = 2.0 * np.pi * (freq[None, :] * np.arange(LX)[:, None] % NX) / NX
    cos, sin = np.cos(angle), np.sin(angle)
    forward = np.zeros((LX, 2, MZ, MX, 2, MZ))
    inverse = np.zeros((MX, 2, MZ, LX, 2, MZ))
    for z in range(MZ):
        forward[:, 0, z, :, 0, z] = cos
        forward[:, 1, z, :, 0, z] = sin
        forward[:, 1, z, :, 1, z] = cos
        forward[:, 0, z, :, 1, z] = -sin
        inverse[:, 0, z, :, 0, z] = cos.T
        inverse[:, 1, z, :, 0, z] = -sin.T
        inverse[:, 1, z, :, 1, z] = cos.T
        inverse[:, 0, z, :, 1, z] = sin.T
    return split(forward.reshape(256, 1024)), split(inverse.reshape(1024, 256))


def spread_table():
    table = np.zeros((9 * C, 3, 3, 256), np.float32)
    for dz in range(3):
        for dy in range(3):
            base = (dy * 3 + dz) * C
            for c in range(C):
                table[base + c, dz, dy, c * LY : (c + 1) * LY] = 1.0
                table[base + c, dz, dy, ROWS + c] = 1.0
                table[base + c, dz, dy, ROWS + 32 + c] = 1.0
    return table.reshape(9 * C, 9 * 256).astype(ml_dtypes.bfloat16)


def edge_table():
    table = np.zeros((64, ROWS), np.float32)
    for c in range(C):
        table[c, c * LY + LY - 1] = 1.0
        table[32 + c, c * LY] = 1.0
    return table.astype(ml_dtypes.bfloat16)


def two_terms(value):
    high = value.astype(BF16)
    return high, (value - high.astype(F32)).astype(BF16)


def dot(a, b):
    return jnp.dot(a, b, preferred_element_type=F32)


def iota(shape, dim):
    return lax.broadcasted_iota(jnp.int32, shape, dim)


def turned(value, low):
    width = value.shape[1]
    return jnp.where(low, pltpu.roll(value, width - MZ, 1), pltpu.roll(value, MZ, 1))


def kernel(
    state, conv_w, bias, z_fwd, edge, x_fwd_hbm, x_inv_hbm, z_inv_hbm, spread_hbm, mix_hbm,
    out,
    x_fwd, x_inv, z_inv, spread, mix,
    cells, edges, band, conv, y_send, y_recv, x_send, x_recv, m_send, m_recv, joined, b_send, b_recv,
    y_inv, w_same, w_cross,
    load_sem, send_sem, recv_sem, halo_send, halo_recv,
):
    gx = lax.axis_index("gx")
    gy = lax.axis_index("gy")

    def along_x(step):
        return lax.rem(gx + step + GX, GX)

    def along_y(step):
        return lax.rem(gy + step + GY, GY)

    pairs = ((x_fwd_hbm, x_fwd), (x_inv_hbm, x_inv), (z_inv_hbm, z_inv), (spread_hbm, spread), (mix_hbm, mix))
    loads = [pltpu.make_async_copy(src, dst, load_sem.at[i]) for i, (src, dst) in enumerate(pairs)]
    for load in loads:
        load.start()

    barrier = pltpu.get_barrier_semaphore()

    @pl.loop(1, GY)
    def _(step):
        pl.semaphore_signal(barrier, inc=1, device_id={"gx": gx, "gy": along_y(step)}, device_id_type=MESH)

    @pl.loop(1, GX)
    def _(step):
        pl.semaphore_signal(barrier, inc=1, device_id={"gx": along_x(step), "gy": gy}, device_id_type=MESH)

    for dx in (-1, 1):
        for dy in (-1, 1):
            pl.semaphore_signal(
                barrier, inc=1, device_id={"gx": along_x(dx), "gy": along_y(dy)}, device_id_type=MESH
            )

    for x in range(LX):
        cells[x + 1, 0:ROWS] = state[:, x].astype(F32).reshape(ROWS, NZ).astype(BF16)
    wide = jnp.concatenate(
        [jnp.concatenate([cells[1 + low, 0:ROWS], cells[5 + low, 0:ROWS]], axis=0) for low in range(4)], axis=1
    )
    z_high, z_low = two_terms(dot(wide, z_fwd[...]))

    row, col = iota((256, 128), 0), iota((256, 128), 1)
    ky = (gy + row // 8) & (MY - 1)
    freq = jnp.where(ky < MY // 2, ky, ky - MY)
    angle = (freq * (gy * LY + (col & 7)) - 64 * (col // 64)) & (NY - 1)
    table = jnp.cos(angle.astype(F32) * (2.0 * math.pi / NY))
    t_high, t_low = two_terms(jnp.where((row & 7) == (col // 8 & 7), table, 0.0))

    def regroup(value):
        return jnp.concatenate(
            [
                jnp.concatenate([value[g * 64 : g * 64 + 64, 0:128], value[g * 64 : g * 64 + 64, 128:256]], axis=0)
                for g in range(5)
            ],
            axis=1,
        )

    z_high, z_low = regroup(z_high), regroup(z_low)
    y_part = dot(
        jnp.concatenate([t_high, t_high, t_low], axis=1), jnp.concatenate([z_high, z_low, z_high], axis=0)
    )
    for g in range(5):
        y_send[:, g * 8 : g * 8 + 8, :] = y_part[:, g * 128 : g * 128 + 128].reshape(GY, 8, 128).astype(BF16)

    pl.semaphore_wait(barrier, PEERS)

    @pl.loop(1, GY)
    def _(step):
        pltpu.make_async_remote_copy(
            src_ref=y_send.at[step],
            dst_ref=y_recv.at[step],
            send_sem=send_sem.at[0],
            recv_sem=recv_sem.at[0],
            device_id={"gx": gx, "gy": along_y(step)},
            device_id_type=MESH,
        ).start()

    for x in range(LX):
        picked = dot(edge[...], cells[x + 1, 0:ROWS]).astype(BF16)
        edges[0, x] = picked[0:32]
        edges[1, x] = picked[32:64]
    left, right = pl.ds(ROWS, 32), pl.ds(ROWS + 32, 32)
    main = pl.ds(0, ROWS)
    inner = pl.ds(1, LX)
    plan = [
        (edges.at[0], cells.at[inner, left], 0, 1),
        (edges.at[1], cells.at[inner, right], 0, -1),
        (cells.at[LX, main], cells.at[0, main], 1, 0),
        (cells.at[1, main], cells.at[LX + 1, main], -1, 0),
        (edges.at[0, LX - 1], cells.at[0, left], 1, 1),
        (edges.at[1, LX - 1], cells.at[0, right], 1, -1),
        (edges.at[0, 0], cells.at[LX + 1, left], -1, 1),
        (edges.at[1, 0], cells.at[LX + 1, right], -1, -1),
    ]
    halos = [
        pltpu.make_async_remote_copy(
            src_ref=src,
            dst_ref=dst,
            send_sem=halo_send.at[i],
            recv_sem=halo_recv.at[i],
            device_id={"gx": along_x(dx), "gy": along_y(dy)},
            device_id_type=MESH,
        )
        for i, (src, dst, dx, dy) in enumerate(plan)
    ]
    for halo in halos:
        halo.start()

    for x in range(LX + 2):
        cells[x, ROWS + 64 : 256] = jnp.zeros((32, NZ), BF16)
    loads[3].wait()
    repeat = (iota((ROWS, C), 0) // LY == iota((ROWS, C), 1)).astype(F32).astype(BF16)
    y_row, cell = iota((ROWS, 256), 0) & 7, iota((ROWS, 256), 1)
    y_col = jnp.where(cell < ROWS, cell & 7, jnp.where(cell < ROWS + 32, -1, jnp.where(cell < ROWS + 64, 8, 100)))
    masks = [y_col == y_row + dy - 1 for dy in range(3)]
    for dx in range(3):
        lines = dot(repeat, conv_w[dx]).astype(BF16)
        for dz in range(3):
            total = jnp.zeros((ROWS, 256), F32)
            for dy in range(3):
                at = (dz * 3 + dy) * 256
                total = jnp.where(masks[dy], dot(lines, spread[:, at : at + 256]), total)
            band[dz * ROWS : (dz + 1) * ROWS, dx * 256 : (dx + 1) * 256] = total.astype(BF16)
    pick = iota((ROWS, C), 0) // LY == iota((ROWS, C), 1)
    bias_rows = jnp.sum(jnp.where(pick, bias[...], 0.0), axis=1, keepdims=True)

    loads[4].wait()
    low20 = (iota((C, 128), 1) & 31) < MZ

    @pl.loop(0, C)
    def _(i):
        lines = jnp.transpose(mix[:, :, i].reshape(128, C))
        w_same[i] = jnp.where(low20, lines, pltpu.roll(lines, MZ, 1))
        w_cross[i] = jnp.where(low20, -pltpu.roll(lines, 128 - MZ, 1), lines)

    row, col = iota((128, 256), 0), iota((128, 256), 1)
    ky = (gy + GY - col // 8) & (MY - 1)
    freq = jnp.where(ky < MY // 2, ky, ky - MY)
    angle = (freq * (gy * LY + (row & 7)) - 64 * (row // 64)) & (NY - 1)
    table = jnp.cos(angle.astype(F32) * (2.0 * math.pi / NY))
    t_high, t_low = two_terms(jnp.where((row // 8 & 7) == (col & 7), table, 0.0))
    y_inv[0] = t_high
    y_inv[1] = t_low

    kx = iota((8, 1024), 1) // 32
    turn = (kx * gx) & 7
    low1 = (iota((8, 1024), 1) & 31) < MZ
    phase_cos = jnp.cos(turn.astype(F32) * (2.0 * math.pi / 8))[0:1]
    phase_sin = jnp.cos(((turn + 6) & 7).astype(F32) * (2.0 * math.pi / 8))
    phase_sin = jnp.where(low1, phase_sin, -phase_sin)[0:1]
    low32 = (iota((32, 1024), 1) & 31) < MZ

    def y_copies():
        return pltpu.make_async_remote_copy(
            src_ref=y_send.at[pl.ds(1, GY - 1)],
            dst_ref=y_recv.at[pl.ds(1, GY - 1)],
            send_sem=send_sem.at[0],
            recv_sem=recv_sem.at[0],
            device_id={"gx": gx, "gy": along_y(1)},
            device_id_type=MESH,
        )

    def x_copies(ref, which):
        return pltpu.make_async_remote_copy(
            src_ref=ref.at[pl.ds(1, GX - 1)],
            dst_ref=ref.at[pl.ds(1, GX - 1)],
            send_sem=send_sem.at[which],
            recv_sem=recv_sem.at[which],
            device_id={"gx": along_x(1), "gy": gy},
            device_id_type=MESH,
        )

    y_copies().wait_recv()
    total = y_send[0].astype(F32)
    for step in range(1, GY):
        total = total + y_recv[step].astype(F32)
    pad = jnp.zeros((12, 256), F32)
    total = jnp.concatenate([jnp.concatenate([total[0:C], total[C:GROUPS]], axis=1), pad], axis=0)
    loads[0].wait()
    s_high, s_low = two_terms(total)
    both = dot(jnp.concatenate([s_high, s_low], axis=0), x_fwd[0])
    x_part = both[0:32] + both[32:64] + dot(s_high, x_fwd[1])
    x_part = x_part * phase_cos + turned(x_part, low32) * phase_sin
    for g in range(GX):
        x_send[g] = x_part[0:24, g * 128 : g * 128 + 128]

    @pl.loop(1, GX)
    def _(step):
        to = along_x(step)
        pltpu.make_async_remote_copy(
            src_ref=x_send.at[to],
            dst_ref=x_recv.at[step],
            send_sem=send_sem.at[1],
            recv_sem=recv_sem.at[1],
            device_id={"gx": to, "gy": gy},
            device_id_type=MESH,
        ).start()

    for halo in halos:
        halo.wait_recv()

    def convolve(x):
        window = cells[pl.ds(x, 3)].reshape(768, NZ)
        taps = dot(band[...], window)
        conv[x] = (
            pltpu.roll(taps[0:ROWS], 1, 1)
            + taps[ROWS : 2 * ROWS]
            + pltpu.roll(taps[2 * ROWS : 3 * ROWS], NZ - 1, 1)
            + bias_rows
        )

    @pl.loop(0, 4)
    def _(x):
        convolve(x)

    x_copies(x_recv, 1).wait_recv()
    modes = x_send[gx]
    for step in range(1, GX):
        modes = modes + x_recv[step]
    crossed = turned(modes, (iota((24, 128), 1) & 31) < MZ)
    mixed = jnp.zeros((C, 128), F32)
    for i in range(C):
        mixed = mixed + w_same[i] * modes[i : i + 1] + w_cross[i] * crossed[i : i + 1]
    m_send[...] = jnp.concatenate([mixed, jnp.zeros((4, 128), F32)], axis=0)

    @pl.loop(1, GX)
    def _(step):
        pltpu.make_async_remote_copy(
            src_ref=m_send,
            dst_ref=m_recv.at[step],
            send_sem=send_sem.at[2],
            recv_sem=recv_sem.at[2],
            device_id={"gx": along_x(step), "gy": gy},
            device_id_type=MESH,
        ).start()

    @pl.loop(4, LX)
    def _(x):
        convolve(x)

    x_copies(m_recv, 2).wait_recv()
    joined[24:32] = jnp.zeros((8, 1024), F32)
    joined[0:24, pl.ds(pl.multiple_of(gx * 128, 128), 128)] = m_send[...]
    for step in range(1, GX):
        joined[0:24, pl.ds(pl.multiple_of(along_x(-step) * 128, 128), 128)] = m_recv[step]
    total = joined[...]
    total = total * phase_cos - turned(total, low32) * phase_sin
    loads[1].wait()
    s_high, s_low = two_terms(total)
    both = dot(jnp.concatenate([s_high, s_low], axis=0), x_inv[0])
    x_back = both[0:32] + both[32:64] + dot(s_high, x_inv[1])
    x_back = jnp.concatenate([x_back[0:C, 0:128], x_back[0:C, 128:256]], axis=0).astype(BF16)
    b_send[...] = x_back
    b_recv[0] = x_back

    @pl.loop(1, GY)
    def _(step):
        pltpu.make_async_remote_copy(
            src_ref=b_send,
            dst_ref=b_recv.at[step],
            send_sem=send_sem.at[3],
            recv_sem=recv_sem.at[3],
            device_id={"gx": gx, "gy": along_y(step)},
            device_id_type=MESH,
        ).start()

    all_b = pltpu.make_async_remote_copy(
        src_ref=b_recv.at[pl.ds(1, GY - 1)],
        dst_ref=b_recv.at[pl.ds(1, GY - 1)],
        send_sem=send_sem.at[3],
        recv_sem=recv_sem.at[3],
        device_id={"gx": gx, "gy": along_y(1)},
        device_id_type=MESH,
    )
    loads[2].wait()
    all_b.wait_recv()
    parts = [b_recv[:, g * 8 : g * 8 + 8, :].astype(F32).reshape(256, 128).astype(BF16) for g in range(5)]
    parts = jnp.concatenate(parts, axis=1)
    back = dot(y_inv[0], parts) + dot(y_inv[1], parts)
    back = jnp.concatenate(
        [
            jnp.concatenate([back[0:64, g * 128 : g * 128 + 128], back[64:128, g * 128 : g * 128 + 128]], axis=1)
            for g in range(5)
        ],
        axis=0,
    )
    u_high, u_low = two_terms(back)
    for low in range(4):
        at = low * NZ
        spectral = (
            dot(u_high, z_inv[0, :, at : at + NZ])
            + dot(u_low, z_inv[0, :, at : at + NZ])
            + dot(u_high, z_inv[1, :, at : at + NZ])
        )
        for high in range(2):
            x = high * 4 + low
            value = conv[x] + spectral[high * ROWS : (high + 1) * ROWS]
            value = jax.nn.gelu(value)
            out[:, x] = value.reshape(C, LY, NZ).astype(BF16)

    y_copies().wait_send()
    for halo in halos:
        halo.wait_send()
    x_copies(x_send, 1).wait_send()
    x_copies(m_recv, 2).wait_send()
    all_b.wait_send()


def on_device(state_field, conv_weight, spectral_weight, channel_bias):
    mix = jnp.transpose(spectral_weight[:, 0], (0, 1, 2, 4, 3))
    x_fwd, x_inv = x_tables()
    vmem, hbm = pl.BlockSpec(memory_space=pltpu.VMEM), pl.BlockSpec(memory_space=pl.ANY)
    return pl.pallas_call(
        kernel,
        out_shape=jax.ShapeDtypeStruct((C, LX, LY, NZ), BF16),
        in_specs=[vmem] * 5 + [hbm] * 5,
        out_specs=vmem,
        scratch_shapes=[
            pltpu.VMEM((2, 256, 1024), BF16),
            pltpu.VMEM((2, 1024, 256), BF16),
            pltpu.VMEM((2, 256, 1024), BF16),
            pltpu.VMEM((9 * C, 9 * 256), BF16),
            pltpu.VMEM((4, 2, C, MZ, C), F32),
            pltpu.VMEM((LX + 2, 256, NZ), BF16),
            pltpu.VMEM((2, LX, 32, NZ), BF16),
            pltpu.VMEM((3 * ROWS, 768), BF16),
            pltpu.VMEM((LX, ROWS, NZ), F32),
            pltpu.VMEM((GY, GROUPS, 128), BF16),
            pltpu.VMEM((GY, GROUPS, 128), BF16),
            pltpu.VMEM((GX, 24, 128), F32),
            pltpu.VMEM((GX, 24, 128), F32),
            pltpu.VMEM((24, 128), F32),
            pltpu.VMEM((GX, 24, 128), F32),
            pltpu.VMEM((32, 1024), F32),
            pltpu.VMEM((GROUPS, 128), BF16),
            pltpu.VMEM((GY, GROUPS, 128), BF16),
            pltpu.VMEM((2, 128, 256), BF16),
            pltpu.VMEM((C, C, 128), F32),
            pltpu.VMEM((C, C, 128), F32),
            pltpu.SemaphoreType.DMA((5,)),
            pltpu.SemaphoreType.DMA((4,)),
            pltpu.SemaphoreType.DMA((4,)),
            pltpu.SemaphoreType.DMA((8,)),
            pltpu.SemaphoreType.DMA((8,)),
        ],
        compiler_params=pltpu.CompilerParams(
            collective_id=0, has_side_effects=True, vmem_limit_bytes=48 * 1024 * 1024
        ),
        cost_estimate=pl.CostEstimate(flops=800_000_000, bytes_accessed=8_000_000, transcendentals=400_000),
    )(
        state_field,
        conv_weight,
        channel_bias.reshape(1, C),
        jnp.asarray(z_forward_table()),
        jnp.asarray(edge_table()),
        jnp.asarray(x_fwd),
        jnp.asarray(x_inv),
        jnp.asarray(z_inverse_table()),
        jnp.asarray(spread_table()),
        mix,
    )


def solution(mesh):
    return jax.shard_map(
        on_device,
        mesh=mesh,
        in_specs=(P(None, "gx", "gy", None), P(), P("gx", "gy", None, None, None, None), P()),
        out_specs=P(None, "gx", "gy", None),
        check_vma=False,
    )
```

```python
import functools
import math

import jax
import jax.numpy as jnp
import ml_dtypes
import numpy as np
from jax import lax
from jax.experimental import pallas as pl
from jax.experimental.pallas import tpu as pltpu
from jax.sharding import PartitionSpec as P

MESH = pl.DeviceIdType.MESH
F32 = jnp.float32
BF16 = jnp.bfloat16
C = 20
NZ = 256
NX = 64
NY = 256
MX = 32
MY = 32
MZ = 16
GX = 8
GY = 32
LX = 8
LY = 8
ROWS = C * LY
GROUPS = 2 * C
PEERS = GX + GY - 2 + 4


def split(table):
    high = table.astype(np.float32).astype(ml_dtypes.bfloat16)
    low = (table - high.astype(np.float64)).astype(np.float32).astype(ml_dtypes.bfloat16)
    return np.stack([high, low])


def z_forward_table():
    z, k = np.arange(NZ)[:, None], np.arange(MZ)[None, :]
    angle = 2.0 * np.pi * (z * k % NZ) / NZ
    cos, sin = np.cos(angle), np.sin(angle)
    table = np.zeros((4, NZ, 2, 4, 2, MZ))
    for low in range(4):
        table[low, :, 0, low, 0] = cos
        table[low, :, 0, low, 1] = -sin
        table[low, :, 1, low, 0] = -sin
        table[low, :, 1, low, 1] = -cos
    return table.reshape(4 * NZ, 256).astype(np.float32).astype(ml_dtypes.bfloat16)


def z_inverse_table():
    k, z = np.arange(MZ)[:, None], np.arange(NZ)[None, :]
    angle = 2.0 * np.pi * (z * k % NZ) / NZ
    weight = np.where(k == 0, 1.0, 2.0) / math.sqrt(float(NX) * NY * NZ * 2.0 * MX * MY * MZ)
    cos, sin = np.cos(angle) * weight, np.sin(angle) * weight
    table = np.zeros((2, 4, 2, MZ, 4, NZ))
    for low in range(4):
        table[0, low, 0, :, low] = cos
        table[0, low, 1, :, low] = -sin
        table[1, low, 0, :, low] = -sin
        table[1, low, 1, :, low] = -cos
    return split(table.reshape(256, 4 * NZ))


def x_tables():
    kx = np.arange(MX)
    freq = np.where(kx < MX // 2, kx, kx - MX)
    angle = 2.0 * np.pi * (freq[None, :] * np.arange(LX)[:, None] % NX) / NX
    cos, sin = np.cos(angle), np.sin(angle)
    forward = np.zeros((LX, 2, MZ, MX, 2, MZ))
    inverse = np.zeros((MX, 2, MZ, LX, 2, MZ))
    for z in range(MZ):
        forward[:, 0, z, :, 0, z] = cos
        forward[:, 1, z, :, 0, z] = sin
        forward[:, 1, z, :, 1, z] = cos
        forward[:, 0, z, :, 1, z] = -sin
        inverse[:, 0, z, :, 0, z] = cos.T
        inverse[:, 1, z, :, 0, z] = -sin.T
        inverse[:, 1, z, :, 1, z] = cos.T
        inverse[:, 0, z, :, 1, z] = sin.T
    return split(forward.reshape(256, 1024)), split(inverse.reshape(1024, 256))


def spread_table():
    table = np.zeros((9 * C, 3, 3, 256), np.float32)
    for dz in range(3):
        for dy in range(3):
            base = (dy * 3 + dz) * C
            for c in range(C):
                table[base + c, dz, dy, c * LY : (c + 1) * LY] = 1.0
                table[base + c, dz, dy, ROWS + c] = 1.0
                table[base + c, dz, dy, ROWS + 32 + c] = 1.0
    return table.reshape(9 * C, 9 * 256).astype(ml_dtypes.bfloat16)


def edge_table():
    table = np.zeros((64, ROWS), np.float32)
    for c in range(C):
        table[c, c * LY + LY - 1] = 1.0
        table[32 + c, c * LY] = 1.0
    return table.astype(ml_dtypes.bfloat16)


def two_terms(value):
    high = value.astype(BF16)
    return high, (value - high.astype(F32)).astype(BF16)


def dot(a, b):
    return jnp.dot(a, b, preferred_element_type=F32)


def iota(shape, dim):
    return lax.broadcasted_iota(jnp.int32, shape, dim)


def turned(value, low):
    width = value.shape[1]
    return jnp.where(low, pltpu.roll(value, width - MZ, 1), pltpu.roll(value, MZ, 1))


def kernel(
    state_hbm, z_fwd_hbm, edge_hbm, x_fwd_hbm, x_inv_hbm, z_inv_hbm, spread_hbm, mix_hbm, conv_w_hbm, bias_hbm,
    out,
    state, z_fwd, edge, x_fwd, x_inv, z_inv, spread, mix, conv_w, bias,
    cells, edges, band, conv, y_send, y_recv, x_send, x_recv, m_send, m_recv, joined, b_send, b_recv,
    y_inv, w_same, w_cross,
    load_sem, send_sem, recv_sem, halo_send, halo_recv,
):
    gx = lax.axis_index("gx")
    gy = lax.axis_index("gy")

    def along_x(step):
        return lax.rem(gx + step + GX, GX)

    def along_y(step):
        return lax.rem(gy + step + GY, GY)

    loads = [
        pltpu.make_async_copy(src, dst, load_sem.at[i])
        for i, (src, dst) in enumerate(
            (
                (state_hbm, state),
                (z_fwd_hbm, z_fwd),
                (edge_hbm, edge),
                (conv_w_hbm, conv_w),
                (spread_hbm, spread),
                (bias_hbm, bias),
                (mix_hbm, mix),
                (x_fwd_hbm, x_fwd),
                (x_inv_hbm, x_inv),
                (z_inv_hbm, z_inv),
            )
        )
    ]
    for load in loads:
        load.start()

    barrier = pltpu.get_barrier_semaphore()

    @pl.loop(1, GY)
    def _(step):
        pl.semaphore_signal(barrier, inc=1, device_id={"gx": gx, "gy": along_y(step)}, device_id_type=MESH)

    @pl.loop(1, GX)
    def _(step):
        pl.semaphore_signal(barrier, inc=1, device_id={"gx": along_x(step), "gy": gy}, device_id_type=MESH)

    for dx in (-1, 1):
        for dy in (-1, 1):
            pl.semaphore_signal(
                barrier, inc=1, device_id={"gx": along_x(dx), "gy": along_y(dy)}, device_id_type=MESH
            )

    row, col = iota((256, 128), 0), iota((256, 128), 1)
    ky = (gy + row // 8) & (MY - 1)
    freq = jnp.where(ky < MY // 2, ky, ky - MY)
    angle = (freq * (gy * LY + (col & 7)) - 64 * (col // 64)) & (NY - 1)
    table = jnp.cos(angle.astype(F32) * (2.0 * math.pi / NY))
    t_high, t_low = two_terms(jnp.where((row & 7) == (col // 8 & 7), table, 0.0))

    loads[0].wait()
    for x in range(LX):
        cells[x + 1, 0:ROWS] = state[:, x].astype(F32).reshape(ROWS, NZ).astype(BF16)
    wide = jnp.concatenate(
        [jnp.concatenate([cells[1 + low, 0:ROWS], cells[5 + low, 0:ROWS]], axis=0) for low in range(4)], axis=1
    )
    loads[1].wait()
    z_high, z_low = two_terms(dot(wide, z_fwd[...]))

    def regroup(value):
        return jnp.concatenate(
            [
                jnp.concatenate([value[g * 64 : g * 64 + 64, 0:128], value[g * 64 : g * 64 + 64, 128:256]], axis=0)
                for g in range(5)
            ],
            axis=1,
        )

    z_high, z_low = regroup(z_high), regroup(z_low)
    y_part = dot(
        jnp.concatenate([t_high, t_high, t_low], axis=1), jnp.concatenate([z_high, z_low, z_high], axis=0)
    )
    for g in range(5):
        y_send[:, g * 8 : g * 8 + 8, :] = y_part[:, g * 128 : g * 128 + 128].reshape(GY, 8, 128).astype(BF16)

    pl.semaphore_wait(barrier, PEERS)

    @pl.loop(1, GY)
    def _(step):
        pltpu.make_async_remote_copy(
            src_ref=y_send.at[step],
            dst_ref=y_recv.at[step],
            send_sem=send_sem.at[0],
            recv_sem=recv_sem.at[0],
            device_id={"gx": gx, "gy": along_y(step)},
            device_id_type=MESH,
        ).start()

    loads[2].wait()
    for x in range(LX):
        picked = dot(edge[...], cells[x + 1, 0:ROWS]).astype(BF16)
        edges[0, x] = picked[0:32]
        edges[1, x] = picked[32:64]
    left, right = pl.ds(ROWS, 32), pl.ds(ROWS + 32, 32)
    main = pl.ds(0, ROWS)
    inner = pl.ds(1, LX)
    plan = [
        (edges.at[0], cells.at[inner, left], 0, 1),
        (edges.at[1], cells.at[inner, right], 0, -1),
        (cells.at[LX, main], cells.at[0, main], 1, 0),
        (cells.at[1, main], cells.at[LX + 1, main], -1, 0),
        (edges.at[0, LX - 1], cells.at[0, left], 1, 1),
        (edges.at[1, LX - 1], cells.at[0, right], 1, -1),
        (edges.at[0, 0], cells.at[LX + 1, left], -1, 1),
        (edges.at[1, 0], cells.at[LX + 1, right], -1, -1),
    ]
    halos = [
        pltpu.make_async_remote_copy(
            src_ref=src,
            dst_ref=dst,
            send_sem=halo_send.at[i],
            recv_sem=halo_recv.at[i],
            device_id={"gx": along_x(dx), "gy": along_y(dy)},
            device_id_type=MESH,
        )
        for i, (src, dst, dx, dy) in enumerate(plan)
    ]
    for halo in halos:
        halo.start()

    for x in range(LX + 2):
        cells[x, ROWS + 64 : 256] = jnp.zeros((32, NZ), BF16)
    loads[3].wait()
    loads[4].wait()
    loads[5].wait()
    repeat = (iota((ROWS, C), 0) // LY == iota((ROWS, C), 1)).astype(F32).astype(BF16)
    y_row, cell = iota((ROWS, 256), 0) & 7, iota((ROWS, 256), 1)
    y_col = jnp.where(cell < ROWS, cell & 7, jnp.where(cell < ROWS + 32, -1, jnp.where(cell < ROWS + 64, 8, 100)))
    masks = [y_col == y_row + dy - 1 for dy in range(3)]
    for dx in range(3):
        lines = dot(repeat, conv_w[dx]).astype(BF16)
        for dz in range(3):
            total = jnp.zeros((ROWS, 256), F32)
            for dy in range(3):
                at = (dz * 3 + dy) * 256
                total = jnp.where(masks[dy], dot(lines, spread[:, at : at + 256]), total)
            band[dz * ROWS : (dz + 1) * ROWS, dx * 256 : (dx + 1) * 256] = total.astype(BF16)
    pick = iota((ROWS, C), 0) // LY == iota((ROWS, C), 1)
    bias_rows = jnp.sum(jnp.where(pick, bias[...], 0.0), axis=1, keepdims=True)

    loads[6].wait()
    low20 = (iota((C, 128), 1) & 31) < MZ

    @pl.loop(0, C)
    def _(i):
        lines = jnp.transpose(mix[:, :, i].reshape(128, C))
        w_same[i] = jnp.where(low20, lines, pltpu.roll(lines, MZ, 1))
        w_cross[i] = jnp.where(low20, -pltpu.roll(lines, 128 - MZ, 1), lines)

    row, col = iota((128, 256), 0), iota((128, 256), 1)
    ky = (gy + GY - col // 8) & (MY - 1)
    freq = jnp.where(ky < MY // 2, ky, ky - MY)
    angle = (freq * (gy * LY + (row & 7)) - 64 * (row // 64)) & (NY - 1)
    table = jnp.cos(angle.astype(F32) * (2.0 * math.pi / NY))
    t_high, t_low = two_terms(jnp.where((row // 8 & 7) == (col & 7), table, 0.0))
    y_inv[0] = t_high
    y_inv[1] = t_low

    kx = iota((8, 1024), 1) // 32
    turn = (kx * gx) & 7
    low1 = (iota((8, 1024), 1) & 31) < MZ
    phase_cos = jnp.cos(turn.astype(F32) * (2.0 * math.pi / 8))[0:1]
    phase_sin = jnp.cos(((turn + 6) & 7).astype(F32) * (2.0 * math.pi / 8))
    phase_sin = jnp.where(low1, phase_sin, -phase_sin)[0:1]
    low32 = (iota((32, 1024), 1) & 31) < MZ

    def y_copies():
        return pltpu.make_async_remote_copy(
            src_ref=y_send.at[pl.ds(1, GY - 1)],
            dst_ref=y_recv.at[pl.ds(1, GY - 1)],
            send_sem=send_sem.at[0],
            recv_sem=recv_sem.at[0],
            device_id={"gx": gx, "gy": along_y(1)},
            device_id_type=MESH,
        )

    def x_copies(ref, which):
        return pltpu.make_async_remote_copy(
            src_ref=ref.at[pl.ds(1, GX - 1)],
            dst_ref=ref.at[pl.ds(1, GX - 1)],
            send_sem=send_sem.at[which],
            recv_sem=recv_sem.at[which],
            device_id={"gx": along_x(1), "gy": gy},
            device_id_type=MESH,
        )

    y_copies().wait_recv()
    total = y_send[0].astype(F32)
    for step in range(1, GY):
        total = total + y_recv[step].astype(F32)
    pad = jnp.zeros((12, 256), F32)
    total = jnp.concatenate([jnp.concatenate([total[0:C], total[C:GROUPS]], axis=1), pad], axis=0)
    loads[7].wait()
    s_high, s_low = two_terms(total)
    both = dot(jnp.concatenate([s_high, s_low], axis=0), x_fwd[0])
    x_part = both[0:32] + both[32:64] + dot(s_high, x_fwd[1])
    x_part = x_part * phase_cos + turned(x_part, low32) * phase_sin
    for g in range(GX):
        x_send[g] = x_part[0:24, g * 128 : g * 128 + 128]

    @pl.loop(1, GX)
    def _(step):
        to = along_x(step)
        pltpu.make_async_remote_copy(
            src_ref=x_send.at[to],
            dst_ref=x_recv.at[step],
            send_sem=send_sem.at[1],
            recv_sem=recv_sem.at[1],
            device_id={"gx": to, "gy": gy},
            device_id_type=MESH,
        ).start()

    for halo in halos:
        halo.wait_recv()

    def convolve(x):
        window = cells[pl.ds(x, 3)].reshape(768, NZ)
        taps = dot(band[...], window)
        conv[x] = (
            pltpu.roll(taps[0:ROWS], 1, 1)
            + taps[ROWS : 2 * ROWS]
            + pltpu.roll(taps[2 * ROWS : 3 * ROWS], NZ - 1, 1)
            + bias_rows
        )

    @pl.loop(0, 4)
    def _(x):
        convolve(x)

    x_copies(x_recv, 1).wait_recv()
    modes = x_send[gx]
    for step in range(1, GX):
        modes = modes + x_recv[step]
    crossed = turned(modes, (iota((24, 128), 1) & 31) < MZ)
    mixed = jnp.zeros((C, 128), F32)
    for i in range(C):
        mixed = mixed + w_same[i] * modes[i : i + 1] + w_cross[i] * crossed[i : i + 1]
    m_send[...] = jnp.concatenate([mixed, jnp.zeros((4, 128), F32)], axis=0)

    @pl.loop(1, GX)
    def _(step):
        pltpu.make_async_remote_copy(
            src_ref=m_send,
            dst_ref=m_recv.at[step],
            send_sem=send_sem.at[2],
            recv_sem=recv_sem.at[2],
            device_id={"gx": along_x(step), "gy": gy},
            device_id_type=MESH,
        ).start()

    @pl.loop(4, LX)
    def _(x):
        convolve(x)

    x_copies(m_recv, 2).wait_recv()
    joined[24:32] = jnp.zeros((8, 1024), F32)
    joined[0:24, pl.ds(pl.multiple_of(gx * 128, 128), 128)] = m_send[...]
    for step in range(1, GX):
        joined[0:24, pl.ds(pl.multiple_of(along_x(-step) * 128, 128), 128)] = m_recv[step]
    total = joined[...]
    total = total * phase_cos - turned(total, low32) * phase_sin
    loads[8].wait()
    s_high, s_low = two_terms(total)
    both = dot(jnp.concatenate([s_high, s_low], axis=0), x_inv[0])
    x_back = both[0:32] + both[32:64] + dot(s_high, x_inv[1])
    x_back = jnp.concatenate([x_back[0:C, 0:128], x_back[0:C, 128:256]], axis=0).astype(BF16)
    b_send[...] = x_back
    b_recv[0] = x_back

    @pl.loop(1, GY)
    def _(step):
        pltpu.make_async_remote_copy(
            src_ref=b_send,
            dst_ref=b_recv.at[step],
            send_sem=send_sem.at[3],
            recv_sem=recv_sem.at[3],
            device_id={"gx": gx, "gy": along_y(step)},
            device_id_type=MESH,
        ).start()

    all_b = pltpu.make_async_remote_copy(
        src_ref=b_recv.at[pl.ds(1, GY - 1)],
        dst_ref=b_recv.at[pl.ds(1, GY - 1)],
        send_sem=send_sem.at[3],
        recv_sem=recv_sem.at[3],
        device_id={"gx": gx, "gy": along_y(1)},
        device_id_type=MESH,
    )
    loads[9].wait()
    all_b.wait_recv()
    parts = [b_recv[:, g * 8 : g * 8 + 8, :].astype(F32).reshape(256, 128).astype(BF16) for g in range(5)]
    parts = jnp.concatenate(parts, axis=1)
    back = dot(y_inv[0], parts) + dot(y_inv[1], parts)
    back = jnp.concatenate(
        [
            jnp.concatenate([back[0:64, g * 128 : g * 128 + 128], back[64:128, g * 128 : g * 128 + 128]], axis=1)
            for g in range(5)
        ],
        axis=0,
    )
    u_high, u_low = two_terms(back)
    for low in range(4):
        at = low * NZ
        spectral = (
            dot(u_high, z_inv[0, :, at : at + NZ])
            + dot(u_low, z_inv[0, :, at : at + NZ])
            + dot(u_high, z_inv[1, :, at : at + NZ])
        )
        for high in range(2):
            x = high * 4 + low
            value = conv[x] + spectral[high * ROWS : (high + 1) * ROWS]
            value = jax.nn.gelu(value)
            out[:, x] = value.reshape(C, LY, NZ).astype(BF16)

    y_copies().wait_send()
    for halo in halos:
        halo.wait_send()
    x_copies(x_send, 1).wait_send()
    x_copies(m_recv, 2).wait_send()
    all_b.wait_send()


def on_device(state_field, conv_weight, spectral_weight, channel_bias):
    mix = jnp.transpose(spectral_weight[:, 0], (0, 1, 2, 4, 3))
    x_fwd, x_inv = x_tables()
    vmem, hbm = pl.BlockSpec(memory_space=pltpu.VMEM), pl.BlockSpec(memory_space=pltpu.HBM)
    return pl.pallas_call(
        kernel,
        out_shape=jax.ShapeDtypeStruct((C, LX, LY, NZ), BF16),
        in_specs=[hbm] * 10,
        out_specs=vmem,
        scratch_shapes=[
            pltpu.VMEM((C, LX, LY, NZ), BF16),
            pltpu.VMEM((4 * NZ, 256), BF16),
            pltpu.VMEM((64, ROWS), BF16),
            pltpu.VMEM((2, 256, 1024), BF16),
            pltpu.VMEM((2, 1024, 256), BF16),
            pltpu.VMEM((2, 256, 1024), BF16),
            pltpu.VMEM((9 * C, 9 * 256), BF16),
            pltpu.VMEM((4, 2, C, MZ, C), F32),
            pltpu.VMEM((3, C, 9 * C), BF16),
            pltpu.VMEM((1, C), F32),
            pltpu.VMEM((LX + 2, 256, NZ), BF16),
            pltpu.VMEM((2, LX, 32, NZ), BF16),
            pltpu.VMEM((3 * ROWS, 768), BF16),
            pltpu.VMEM((LX, ROWS, NZ), F32),
            pltpu.VMEM((GY, GROUPS, 128), BF16),
            pltpu.VMEM((GY, GROUPS, 128), BF16),
            pltpu.VMEM((GX, 24, 128), F32),
            pltpu.VMEM((GX, 24, 128), F32),
            pltpu.VMEM((24, 128), F32),
            pltpu.VMEM((GX, 24, 128), F32),
            pltpu.VMEM((32, 1024), F32),
            pltpu.VMEM((GROUPS, 128), BF16),
            pltpu.VMEM((GY, GROUPS, 128), BF16),
            pltpu.VMEM((2, 128, 256), BF16),
            pltpu.VMEM((C, C, 128), F32),
            pltpu.VMEM((C, C, 128), F32),
            pltpu.SemaphoreType.DMA((10,)),
            pltpu.SemaphoreType.DMA((4,)),
            pltpu.SemaphoreType.DMA((4,)),
            pltpu.SemaphoreType.DMA((8,)),
            pltpu.SemaphoreType.DMA((8,)),
        ],
        compiler_params=pltpu.CompilerParams(
            collective_id=0, has_side_effects=True, vmem_limit_bytes=60 * 1024 * 1024
        ),
        cost_estimate=pl.CostEstimate(flops=800_000_000, bytes_accessed=8_000_000, transcendentals=400_000),
    )(
        state_field,
        jnp.asarray(z_forward_table()),
        jnp.asarray(edge_table()),
        jnp.asarray(x_fwd),
        jnp.asarray(x_inv),
        jnp.asarray(z_inverse_table()),
        jnp.asarray(spread_table()),
        mix,
        conv_weight,
        channel_bias.reshape(1, C),
    )


def solution(mesh):
    return jax.shard_map(
        on_device,
        mesh=mesh,
        in_specs=(P(None, "gx", "gy", None), P(), P("gx", "gy", None, None, None, None), P()),
        out_specs=P(None, "gx", "gy", None),
        check_vma=False,
    )
```

```python
import functools
import math

import jax
import jax.numpy as jnp
import ml_dtypes
import numpy as np
from jax import lax
from jax.experimental import pallas as pl
from jax.experimental.pallas import tpu as pltpu
from jax.sharding import PartitionSpec as P

MESH = pl.DeviceIdType.MESH
F32 = jnp.float32
BF16 = jnp.bfloat16
C = 20
NZ = 256
NX = 64
NY = 256
MX = 32
MY = 32
MZ = 16
GX = 8
GY = 32
LX = 8
LY = 8
ROWS = C * LY
GROUPS = 2 * C
SAME = GY // 2
PEERS = (SAME - 1) + 2 + (GX - 1) + 4
X_FWD = 4 * NZ
EARLY = 5
FAR_Y = (4, 12, 3, 5, 11, 13, 2, 6, 10, 14, 8, 1, 7, 9, 15)
FAR_X = (4, 3, 5, 2, 6, 1, 7)
X_INV = X_FWD + 2048
Z_INV = X_INV + 2048


def split(table):
    high = table.astype(np.float32).astype(ml_dtypes.bfloat16)
    low = (table - high.astype(np.float64)).astype(np.float32).astype(ml_dtypes.bfloat16)
    return np.stack([high, low])


def z_forward_table():
    z, k = np.arange(NZ)[:, None], np.arange(MZ)[None, :]
    angle = 2.0 * np.pi * (z * k % NZ) / NZ
    cos, sin = np.cos(angle), np.sin(angle)
    table = np.zeros((4, NZ, 2, 4, 2, MZ))
    for low in range(4):
        table[low, :, 0, low, 0] = cos
        table[low, :, 0, low, 1] = -sin
        table[low, :, 1, low, 0] = -sin
        table[low, :, 1, low, 1] = -cos
    return table.reshape(4 * NZ, 256).astype(np.float32).astype(ml_dtypes.bfloat16)


def z_inverse_table():
    k, z = np.arange(MZ)[:, None], np.arange(NZ)[None, :]
    angle = 2.0 * np.pi * (z * k % NZ) / NZ
    weight = np.where(k == 0, 1.0, 2.0) / math.sqrt(float(NX) * NY * NZ * 2.0 * MX * MY * MZ)
    cos, sin = np.cos(angle) * weight, np.sin(angle) * weight
    table = np.zeros((2, 4, 2, MZ, 4, NZ))
    for low in range(4):
        table[0, low, 0, :, low] = cos
        table[0, low, 1, :, low] = -sin
        table[1, low, 0, :, low] = -sin
        table[1, low, 1, :, low] = -cos
    return split(table.reshape(256, 4 * NZ))


def x_tables():
    kx = np.arange(MX)
    freq = np.where(kx < MX // 2, kx, kx - MX)
    angle = 2.0 * np.pi * (freq[None, :] * np.arange(LX)[:, None] % NX) / NX
    cos, sin = np.cos(angle), np.sin(angle)
    forward = np.zeros((LX, 2, MZ, MX, 2, MZ))
    inverse = np.zeros((MX, 2, MZ, LX, 2, MZ))
    for z in range(MZ):
        forward[:, 0, z, :, 0, z] = cos
        forward[:, 1, z, :, 0, z] = sin
        forward[:, 1, z, :, 1, z] = cos
        forward[:, 0, z, :, 1, z] = -sin
        inverse[:, 0, z, :, 0, z] = cos.T
        inverse[:, 1, z, :, 0, z] = -sin.T
        inverse[:, 1, z, :, 1, z] = cos.T
        inverse[:, 0, z, :, 1, z] = sin.T
    return split(forward.reshape(256, 1024)), split(inverse.reshape(1024, 256))


def spread_table():
    table = np.zeros((9 * C, 3, 3, 256), np.float32)
    for dz in range(3):
        for dy in range(3):
            base = (dy * 3 + dz) * C
            for c in range(C):
                table[base + c, dz, dy, c * LY : (c + 1) * LY] = 1.0
                table[base + c, dz, dy, ROWS + c] = 1.0
                table[base + c, dz, dy, ROWS + 32 + c] = 1.0
    return table.reshape(9 * C, 9 * 256).astype(ml_dtypes.bfloat16)


def tables():
    x_fwd, x_inv = x_tables()
    blocks = [z_forward_table()]
    blocks += [x_fwd[term, :, n * 256 : n * 256 + 256] for term in range(2) for n in range(4)]
    blocks += [x_inv[0], x_inv[1]]
    z_inv = z_inverse_table()
    blocks += [z_inv[term, :, n * 256 : n * 256 + 256] for term in range(2) for n in range(4)]
    return np.concatenate(blocks, axis=0)


def two_terms(value):
    high = value.astype(BF16)
    return high, (value - high.astype(F32)).astype(BF16)


def dot(a, b):
    return jnp.dot(a, b, preferred_element_type=F32)


def iota(shape, dim):
    return lax.broadcasted_iota(jnp.int32, shape, dim)


def turned(value, low):
    width = value.shape[1]
    return jnp.where(low, pltpu.roll(value, width - MZ, 1), pltpu.roll(value, MZ, 1))


def kernel(
    state_hbm, tables_hbm, small_hbm, spread_hbm, mix_hbm,
    out,
    state, table, small, spread, mix,
    cells, edges, band, conv, z_send, z_recv, y_send, y_recv, x_send, x_recv, m_send, m_recv, joined, b_send, b_recv,
    y_inv, w_same, w_cross,
    load_sem, send_sem, recv_sem, b_send_sem, b_recv_sem, halo_send, halo_recv,
):
    gx = lax.axis_index("gx")
    gy = lax.axis_index("gy")

    def along_x(step):
        return lax.rem(gx + step + GX, GX)

    def along_y(step):
        return lax.rem(gy + step + GY, GY)

    core = lax.rem(gy, 2)
    other = gy + 1 - 2 * core

    barrier = pltpu.get_barrier_semaphore()
    peers = [(0, 2 * step) for step in FAR_Y] + [(dx, dy) for dy in (-1, 1) for dx in (-1, 0, 1)]
    peers += [(step, 0) for step in FAR_X]
    for dx, dy in peers:
        pl.semaphore_signal(
            barrier, inc=1, device_id={"gx": along_x(dx), "gy": along_y(dy)}, device_id_type=MESH
        )

    def rows_of_table(first, count):
        return tables_hbm.at[pl.ds(first, count)], table.at[pl.ds(first, count)]

    loads = [
        pltpu.make_async_copy(src, dst, load_sem.at[i])
        for i, (src, dst) in enumerate(
            (
                (state_hbm, state),
                rows_of_table(0, X_FWD),
                (small_hbm, small),
                (spread_hbm, spread),
                (mix_hbm, mix),
                rows_of_table(X_FWD, 2048),
                rows_of_table(X_INV, 2048),
                rows_of_table(Z_INV, 2048),
            )
        )
    ]
    for load in loads:
        load.start()

    row, col = iota((128, 256), 0), iota((128, 256), 1)
    ky = (gy + row // 8 * 2) & (MY - 1)
    freq = jnp.where(ky < MY // 2, ky, ky - MY)
    place = jnp.where(col < 128, gy, other) * LY + (col & 7)
    angle = (freq * place - (col & 64)) & (NY - 1)
    turns = jnp.cos(angle.astype(F32) * (2.0 * math.pi / NY))
    t_high, t_low = two_terms(jnp.where((row & 7) == (col // 8 & 7), turns, 0.0))

    loads[0].wait()
    for x in range(LX):
        cells[x + 1, 0:ROWS] = state[:, x].astype(F32).reshape(ROWS, NZ).astype(BF16)
    wide = jnp.concatenate(
        [jnp.concatenate([cells[1 + low, 0:ROWS], cells[5 + low, 0:ROWS]], axis=0) for low in range(4)], axis=1
    )
    loads[1].wait()
    spectrum = dot(wide, table[0:X_FWD])

    def regroup(value, first):
        return jnp.concatenate([value[g * 64 : g * 64 + 64, first : first + 128] for g in range(5)], axis=1)

    plain, crossed = regroup(spectrum, 0), regroup(spectrum, 128)
    z_send[...] = plain
    pl.semaphore_wait(barrier, PEERS)
    exchange = pltpu.make_async_remote_copy(
        src_ref=z_send,
        dst_ref=z_recv,
        send_sem=send_sem.at[4],
        recv_sem=recv_sem.at[4],
        device_id={"gx": gx, "gy": other},
        device_id_type=MESH,
    )
    exchange.start()

    left, right = pl.ds(ROWS, 32), pl.ds(ROWS + 32, 32)
    main = pl.ds(0, ROWS)
    inner = pl.ds(1, LX)
    plan = [
        (edges.at[0], cells.at[inner, left], 0, 1),
        (edges.at[1], cells.at[inner, right], 0, -1),
        (cells.at[LX, main], cells.at[0, main], 1, 0),
        (cells.at[1, main], cells.at[LX + 1, main], -1, 0),
        (edges.at[0, LX - 1], cells.at[0, left], 1, 1),
        (edges.at[1, LX - 1], cells.at[0, right], 1, -1),
        (edges.at[0, 0], cells.at[LX + 1, left], -1, 1),
        (edges.at[1, 0], cells.at[LX + 1, right], -1, -1),
    ]
    halos = [
        pltpu.make_async_remote_copy(
            src_ref=src,
            dst_ref=dst,
            send_sem=halo_send.at[i],
            recv_sem=halo_recv.at[i],
            device_id={"gx": along_x(dx), "gy": along_y(dy)},
            device_id_type=MESH,
        )
        for i, (src, dst, dx, dy) in enumerate(plan)
    ]
    for halo in halos[2:4]:
        halo.start()

    def y_product(plain, crossed, first):
        high, low = two_terms(jnp.concatenate([plain, crossed], axis=0))
        left_high, left_low = t_high[:, first : first + 128], t_low[:, first : first + 128]
        return dot(
            jnp.concatenate([left_high, left_high, left_low], axis=1), jnp.concatenate([high, low, high], axis=0)
        )

    y_part = y_product(plain, crossed, 0)
    exchange.wait_recv()
    plain = z_recv[...]
    low64 = (iota((64, 640), 1) & 31) < MZ
    crossed = jnp.where(low64, pltpu.roll(plain, 640 - MZ, 1), -pltpu.roll(plain, MZ, 1))
    y_part = y_part + y_product(plain, crossed, 128)
    for g in range(5):
        y_send[:, g * 8 : g * 8 + 8, :] = y_part[:, g * 128 : g * 128 + 128].reshape(SAME, 8, 128).astype(BF16)

    for step in FAR_Y:
        pltpu.make_async_remote_copy(
            src_ref=y_send.at[step],
            dst_ref=y_recv.at[step],
            send_sem=send_sem.at[0],
            recv_sem=recv_sem.at[0],
            device_id={"gx": gx, "gy": along_y(2 * step)},
            device_id_type=MESH,
        ).start()

    row, col = iota((64, ROWS), 0), iota((64, ROWS), 1)
    last = jnp.where(row < C, row * LY + LY - 1, -1)
    first = jnp.where(row - 32 < C, (row - 32) * LY, -1)
    edge = (col == jnp.where(row < 32, last, first)).astype(F32).astype(BF16)
    for x in range(LX):
        picked = dot(edge, cells[x + 1, 0:ROWS]).astype(BF16)
        edges[0, x] = picked[0:32]
        edges[1, x] = picked[32:64]
    for halo in halos[:2] + halos[4:]:
        halo.start()

    for x in range(LX + 2):
        cells[x, ROWS + 64 : 256] = jnp.zeros((32, NZ), BF16)
    loads[2].wait()
    loads[3].wait()
    repeat = (iota((ROWS, C), 0) // LY == iota((ROWS, C), 1)).astype(F32).astype(BF16)
    y_row, cell = iota((ROWS, 256), 0) & 7, iota((ROWS, 256), 1)
    y_col = jnp.where(cell < ROWS, cell & 7, jnp.where(cell < ROWS + 32, -1, jnp.where(cell < ROWS + 64, 8, 100)))
    masks = [y_col == y_row + dy - 1 for dy in range(3)]
    for dx in range(3):
        lines = dot(repeat, small[dx, 0:C].astype(BF16)).astype(BF16)[:, 0 : 9 * C]
        for dz in range(3):
            total = jnp.zeros((ROWS, 256), F32)
            for dy in range(3):
                at = (dz * 3 + dy) * 256
                total = jnp.where(masks[dy], dot(lines, spread[:, at : at + 256]), total)
            band[dz * ROWS : (dz + 1) * ROWS, dx * 256 : (dx + 1) * 256] = total.astype(BF16)
    pick = iota((ROWS, C), 0) // LY == iota((ROWS, C), 1)
    bias_rows = jnp.sum(jnp.where(pick, small[0, 24:25, 0:C], 0.0), axis=1, keepdims=True)

    loads[4].wait()
    low20 = (iota((C, 128), 1) & 31) < MZ

    @pl.loop(0, C)
    def _(i):
        lines = jnp.transpose(mix[:, :, i].reshape(128, C))
        w_same[i] = jnp.where(low20, lines, pltpu.roll(lines, MZ, 1))
        w_cross[i] = jnp.where(low20, -pltpu.roll(lines, 128 - MZ, 1), lines)

    row, col = iota((128, 256), 0), iota((128, 256), 1)
    ky = (jnp.where(col < 128, gy, other) + GY - 2 * (col // 8 & (SAME - 1))) & (MY - 1)
    freq = jnp.where(ky < MY // 2, ky, ky - MY)
    angle = (freq * (gy * LY + (row & 7)) - 64 * (row // 64)) & (NY - 1)
    turns = jnp.cos(angle.astype(F32) * (2.0 * math.pi / NY))
    t_high, t_low = two_terms(jnp.where((row // 8 & 7) == (col & 7), turns, 0.0))
    y_inv[0] = t_high
    y_inv[1] = t_low

    kx = iota((8, 1024), 1) // 32
    turn = (kx * gx) & 7
    low1 = (iota((8, 1024), 1) & 31) < MZ
    phase_cos = jnp.cos(turn.astype(F32) * (2.0 * math.pi / 8))[0:1]
    phase_sin = jnp.cos(((turn + 6) & 7).astype(F32) * (2.0 * math.pi / 8))
    phase_sin = jnp.where(low1, phase_sin, -phase_sin)[0:1]
    low32 = (iota((32, 1024), 1) & 31) < MZ

    def y_copies():
        return pltpu.make_async_remote_copy(
            src_ref=y_send.at[pl.ds(1, SAME - 1)],
            dst_ref=y_recv.at[pl.ds(1, SAME - 1)],
            send_sem=send_sem.at[0],
            recv_sem=recv_sem.at[0],
            device_id={"gx": gx, "gy": along_y(2)},
            device_id_type=MESH,
        )

    def x_copies(ref, which):
        return pltpu.make_async_remote_copy(
            src_ref=ref.at[pl.ds(1, GX - 1)],
            dst_ref=ref.at[pl.ds(1, GX - 1)],
            send_sem=send_sem.at[which],
            recv_sem=recv_sem.at[which],
            device_id={"gx": along_x(1), "gy": gy},
            device_id_type=MESH,
        )

    y_copies().wait_recv()
    total = y_send[0].astype(F32)
    for step in range(1, SAME):
        total = total + y_recv[step].astype(F32)
    pad = jnp.zeros((12, 256), F32)
    total = jnp.concatenate([jnp.concatenate([total[0:C], total[C:GROUPS]], axis=1), pad], axis=0)
    loads[5].wait()
    s_high, s_low = two_terms(total)
    s_both = jnp.concatenate([s_high, s_low], axis=0)

    def x_block(term, n):
        at = X_FWD + (term * 4 + n) * 256
        return table[at : at + 256]

    both = jnp.concatenate([dot(s_both, x_block(0, n)) for n in range(4)], axis=1)
    x_part = both[0:32] + both[32:64] + jnp.concatenate([dot(s_high, x_block(1, n)) for n in range(4)], axis=1)
    x_part = x_part * phase_cos + turned(x_part, low32) * phase_sin
    for g in range(GX):
        x_send[g] = x_part[0:24, g * 128 : g * 128 + 128]

    for step in FAR_X:
        to = along_x(step)
        pltpu.make_async_remote_copy(
            src_ref=x_send.at[to],
            dst_ref=x_recv.at[step],
            send_sem=send_sem.at[1],
            recv_sem=recv_sem.at[1],
            device_id={"gx": to, "gy": gy},
            device_id_type=MESH,
        ).start()

    x_copies(x_recv, 1).wait_recv()
    modes = x_send[gx]
    for step in range(1, GX):
        modes = modes + x_recv[step]
    crossed = turned(modes, (iota((24, 128), 1) & 31) < MZ)
    mixed = jnp.zeros((C, 128), F32)
    for i in range(C):
        mixed = mixed + w_same[i] * modes[i : i + 1] + w_cross[i] * crossed[i : i + 1]
    m_send[...] = jnp.concatenate([mixed, jnp.zeros((4, 128), F32)], axis=0)

    for step in FAR_X:
        pltpu.make_async_remote_copy(
            src_ref=m_send,
            dst_ref=m_recv.at[step],
            send_sem=send_sem.at[2],
            recv_sem=recv_sem.at[2],
            device_id={"gx": along_x(step), "gy": gy},
            device_id_type=MESH,
        ).start()

    for halo in halos:
        halo.wait_recv()

    def convolve(x):
        window = cells[pl.ds(x, 3)].reshape(768, NZ)
        taps = dot(band[...], window)
        conv[x] = (
            pltpu.roll(taps[0:ROWS], 1, 1)
            + taps[ROWS : 2 * ROWS]
            + pltpu.roll(taps[2 * ROWS : 3 * ROWS], NZ - 1, 1)
            + bias_rows
        )

    @pl.loop(0, EARLY)
    def _(x):
        convolve(x)

    x_copies(m_recv, 2).wait_recv()
    joined[24:32] = jnp.zeros((8, 1024), F32)
    joined[0:24, pl.ds(pl.multiple_of(gx * 128, 128), 128)] = m_send[...]
    for step in range(1, GX):
        joined[0:24, pl.ds(pl.multiple_of(along_x(-step) * 128, 128), 128)] = m_recv[step]
    total = joined[...]
    total = total * phase_cos - turned(total, low32) * phase_sin
    loads[6].wait()
    s_high, s_low = two_terms(total)
    both = dot(jnp.concatenate([s_high, s_low], axis=0), table[X_INV : X_INV + 1024])
    x_back = both[0:32] + both[32:64] + dot(s_high, table[X_INV + 1024 : X_INV + 2048])
    x_back = jnp.concatenate([x_back[0:C, 0:128], x_back[0:C, 128:256]], axis=0).astype(BF16)
    b_send[0] = x_back
    b_recv[0] = x_back

    def to_other(src, first, count, which):
        return pltpu.make_async_remote_copy(
            src_ref=src,
            dst_ref=b_recv.at[pl.ds(first, count)],
            send_sem=send_sem.at[which],
            recv_sem=recv_sem.at[which],
            device_id={"gx": gx, "gy": other},
            device_id_type=MESH,
        )

    def b_copy(step):
        return pltpu.make_async_remote_copy(
            src_ref=b_send.at[0],
            dst_ref=b_recv.at[step],
            send_sem=b_send_sem.at[step],
            recv_sem=b_recv_sem.at[step],
            device_id={"gx": gx, "gy": along_y(2 * step)},
            device_id_type=MESH,
        )

    for step in FAR_Y:
        b_copy(step).start()

    handed = [to_other(b_send, SAME, 1, 3)]
    handed[0].start()

    @pl.loop(EARLY, LX)
    def _(x):
        convolve(x)

    for step in reversed(FAR_Y):
        b_copy(step).wait_recv()
        handed.append(to_other(b_recv.at[pl.ds(step, 1)], SAME + step, 1, 4 + step))
        handed[-1].start()

    loads[7].wait()
    for copy in handed:
        copy.wait_recv()
    parts = [b_recv[:, g * 8 : g * 8 + 8, :].astype(F32).reshape(256, 128).astype(BF16) for g in range(5)]
    parts = jnp.concatenate(parts, axis=1)
    back = dot(y_inv[0], parts) + dot(y_inv[1], parts)
    back = jnp.concatenate(
        [
            jnp.concatenate([back[0:64, g * 128 : g * 128 + 128], back[64:128, g * 128 : g * 128 + 128]], axis=1)
            for g in range(5)
        ],
        axis=0,
    )
    u_high, u_low = two_terms(back)
    for low in range(4):
        at = Z_INV + low * 256
        rough, fine = table[at : at + 256], table[at + 1024 : at + 1280]
        spectral = dot(u_high, rough) + dot(u_low, rough) + dot(u_high, fine)
        for high in range(2):
            x = high * 4 + low
            value = conv[x] + spectral[high * ROWS : (high + 1) * ROWS]
            value = jax.nn.gelu(value)
            out[:, x] = value.reshape(C, LY, NZ).astype(BF16)

    y_copies().wait_send()
    for halo in halos:
        halo.wait_send()
    x_copies(x_send, 1).wait_send()
    x_copies(m_recv, 2).wait_send()
    exchange.wait_send()
    for step in FAR_Y:
        b_copy(step).wait_send()
    for copy in handed:
        copy.wait_send()


def on_device(state_field, conv_weight, spectral_weight, channel_bias):
    mix = jnp.transpose(spectral_weight[:, 0], (0, 1, 2, 4, 3))
    small = jnp.pad(conv_weight.astype(F32), ((0, 0), (0, 32 - C), (0, 256 - 9 * C)))
    small = small + jnp.pad(channel_bias.reshape(1, 1, C), ((0, 2), (24, 7), (0, 256 - C)))
    vmem, hbm = pl.BlockSpec(memory_space=pltpu.VMEM), pl.BlockSpec(memory_space=pltpu.HBM)
    return pl.pallas_call(
        kernel,
        out_shape=jax.ShapeDtypeStruct((C, LX, LY, NZ), BF16),
        in_specs=[hbm] * 5,
        out_specs=vmem,
        scratch_shapes=[
            pltpu.VMEM((C, LX, LY, NZ), BF16),
            pltpu.VMEM((Z_INV + 2048, 256), BF16),
            pltpu.VMEM((3, 32, 256), F32),
            pltpu.VMEM((9 * C, 9 * 256), BF16),
            pltpu.VMEM((4, 2, C, MZ, C), F32),
            pltpu.VMEM((LX + 2, 256, NZ), BF16),
            pltpu.VMEM((2, LX, 32, NZ), BF16),
            pltpu.VMEM((3 * ROWS, 768), BF16),
            pltpu.VMEM((LX, ROWS, NZ), F32),
            pltpu.VMEM((64, 640), F32),
            pltpu.VMEM((64, 640), F32),
            pltpu.VMEM((SAME, GROUPS, 128), BF16),
            pltpu.VMEM((SAME, GROUPS, 128), BF16),
            pltpu.VMEM((GX, 24, 128), F32),
            pltpu.VMEM((GX, 24, 128), F32),
            pltpu.VMEM((24, 128), F32),
            pltpu.VMEM((GX, 24, 128), F32),
            pltpu.VMEM((32, 1024), F32),
            pltpu.VMEM((1, GROUPS, 128), BF16),
            pltpu.VMEM((GY, GROUPS, 128), BF16),
            pltpu.VMEM((2, 128, 256), BF16),
            pltpu.VMEM((C, C, 128), F32),
            pltpu.VMEM((C, C, 128), F32),
            pltpu.SemaphoreType.DMA((8,)),
            pltpu.SemaphoreType.DMA((20,)),
            pltpu.SemaphoreType.DMA((20,)),
            pltpu.SemaphoreType.DMA((SAME,)),
            pltpu.SemaphoreType.DMA((SAME,)),
            pltpu.SemaphoreType.DMA((8,)),
            pltpu.SemaphoreType.DMA((8,)),
        ],
        compiler_params=pltpu.CompilerParams(
            collective_id=0, has_side_effects=True, vmem_limit_bytes=54000 * 1024
        ),
        cost_estimate=pl.CostEstimate(flops=800_000_000, bytes_accessed=8_000_000, transcendentals=400_000),
    )(
        state_field,
        jnp.asarray(tables()),
        small,
        jnp.asarray(spread_table()),
        mix,
    )


def solution(mesh):
    return jax.shard_map(
        on_device,
        mesh=mesh,
        in_specs=(P(None, "gx", "gy", None), P(), P("gx", "gy", None, None, None, None), P()),
        out_specs=P(None, "gx", "gy", None),
        check_vma=False,
    )
```
